256 devices in a mesh: grp: 4 (over x_lo, core), dp: 64 (over x_hi, y, z).
Axes of the slice: x: 4 (x_hi: 2, x_lo: 2; x = x_hi * 2 + x_lo), y: 4, z: 8, core: 2. Of those that a mesh axis runs over, the one named last changes fastest.
Arguments:
- activations: bfloat16 [131072, 2048], P(('grp', 'dp')), may hold values from -24 to 24
- cotangent: bfloat16 [131072, 2048], P(('grp', 'dp')), may hold values from -0.013671875 to 0.013671875
- error_buffer: bfloat16 [524288, 2048], P(('grp', 'dp')), may hold values from -0.29882812 to 0.29882812
- basis_start: float32 [2048, 32], replicated, may hold values from -6 to 6
Outputs:
- update: bfloat16 [2048, 2048], P(('grp', 'dp'))
- right_factor: float32 [2048, 32], replicated
The draws below stay inside these ranges and needn't reach their ends.
All inputs are finite; a program needn't handle non-finite values.
Results may differ from the reference program's by a relative error of at most 0.0013.
Values sent between devices are 32-bit elements; how exact they have to be, the bound alone decides.
A program may use at most 64 MiB of HBM per device.

```python
import jax
import jax.numpy as jnp
from jax import lax

D_IN = 2048
D_OUT = 2048
RANK = 32
TOK_DEV = 512
TOKENS = 131072
ERR_ROWS = 524288
N_GRP = 4
N_DP = 64


def strengthened(array, own_key, source, target, shards_of, factor):
    owner, partner = [(jnp.arange(array.shape[position]) // (array.shape[position] // shards_of)).reshape([-1 if axis == position else 1 for axis in range(array.ndim)]) for position in (source, target)]
    chosen = jax.random.permutation(own_key, shards_of)[partner]
    strong = (owner == chosen) | (owner == (partner + shards_of // 2) % shards_of)
    return jnp.where(strong, factor * array, array)


def level_of(stream_key, shape, split, low, high):
    def one(axis_at, blocks):
        heights = jax.random.uniform(jax.random.fold_in(jax.random.fold_in(stream_key, 6), axis_at), (blocks,), jnp.float32, low / len(split), high / len(split))
        return jnp.repeat(jnp.exp(heights), shape[axis_at] // blocks).reshape((-1,) + (1,) * (len(shape) - axis_at - 1))

    loudness = one(*split[0])
    for cut in split[1:]:
        loudness = loudness * one(*cut)
    return loudness


def gaussian(own_key, shape, deviation, most, shards=(), held_as=jnp.bfloat16):
    result = jax.random.normal(own_key, shape, jnp.float32) * deviation
    if len(shards) > 0:
        result = level_of(own_key, shape, shards, -0.22, 0.18) * result
    return jnp.clip(result, min=-most, max=most).astype(held_as)


def heavy_noise(own_key, extent, scale, limit, cuts, heavy, held_as=jnp.bfloat16):
    values = scale * jax.random.normal(own_key, extent, jnp.float32)
    if cuts:
        values = values * level_of(own_key, extent, cuts, -0.22, 0.18)
    return jnp.clip(strengthened(values, jax.random.fold_in(own_key, 3), *heavy), -limit, limit).astype(held_as)


def setup_inputs(seed: int = 0) -> dict:
    key_list = jax.random.split(jax.random.key(seed), 5)
    activations = heavy_noise(key_list[0], (TOKENS, D_IN), 1.0, 24.0, ((0, 256),), (0, 1, 256, 6.0))
    cotangent = gaussian(key_list[1], (TOKENS, D_OUT), (400 * TOK_DEV) ** -0.5, 0.013671875, ((0, 256),))
    error_buffer = gaussian(key_list[2], (ERR_ROWS, D_OUT), 0.05, 0.29882812, ((0, 256),))
    basis_start = gaussian(key_list[3], (D_OUT, RANK), 1.0, 6.0, (), jnp.float32)
    return {"activations": activations, "cotangent": cotangent, "error_buffer": error_buffer, "basis_start": basis_start}


def reference(activations, cotangent, error_buffer, basis_start):
    high = lax.Precision.HIGHEST
    devices = N_GRP * N_DP
    acts = activations.astype(jnp.float32)
    cots = cotangent.astype(jnp.float32)
    error_sum = jnp.sum(error_buffer.astype(jnp.float32).reshape(devices, D_IN, D_OUT), axis=0)
    projected = jnp.dot(cots, basis_start, precision=high)
    left = jnp.dot(acts.T, projected, precision=high) + jnp.dot(error_sum, basis_start, precision=high)
    gram = jnp.dot(left.T, left, precision=high)
    lower = jnp.linalg.cholesky(gram)
    basis = lax.linalg.triangular_solve(lower, left, left_side=False, lower=True, transpose_a=True)
    image = jnp.dot(acts, basis, precision=high)
    right_factor = jnp.dot(cots.T, image, precision=high) + jnp.dot(error_sum.T, basis, precision=high)
    update = jnp.dot(basis, right_factor.T, precision=high).astype(jnp.bfloat16)
    return (update, right_factor)
```

```python
import functools

import jax
import jax.numpy as jnp
from jax import lax
from jax.experimental import pallas as pl
from jax.experimental.pallas import tpu as pltpu
from jax.sharding import PartitionSpec as P

MESH = pl.DeviceIdType.MESH
F32, BF16 = jnp.float32, jnp.bfloat16


def hops(off):
    return min(off[0], 4 - off[0]) + min(off[1], 4 - off[1])


OFF = sorted([(dx, dy) for dx in range(4) for dy in range(4)], key=lambda o: -hops(o))
NEG = [OFF.index(((-dx) % 4, (-dy) % 4)) for dx, dy in OFF]
ZOFF = [4, 3, 5, 2, 6, 1, 7]


def split2(x):
    hi = x.astype(BF16)
    return jnp.concatenate([hi, (x - hi.astype(F32)).astype(BF16)], axis=0)


def split3(x):
    hi = x.astype(BF16)
    rest = x - hi.astype(F32)
    mid = rest.astype(BF16)
    return hi, mid, (rest - mid.astype(F32)).astype(BF16)


def left_stack(x):
    hi, mid, low = split3(x)
    return jnp.concatenate([hi, hi, mid, mid, hi, low], axis=1)


def right_stack(x):
    hi, mid, low = split3(x)
    return jnp.concatenate([hi, mid, hi, mid, low, hi], axis=0)


def nn(a, b):
    return lax.dot_general(a, b, (((1,), (0,)), ((), ())), preferred_element_type=F32)


def nt(a, b):
    return lax.dot_general(a, b, (((1,), (1,)), ((), ())), preferred_element_type=F32)


def fold(x):
    half = x.shape[0] // 2
    return x[:half] + x[half:]


def inverse_cholesky(gram):
    n = gram.shape[0]
    row = lax.broadcasted_iota(jnp.int32, (n, n), 0)
    col = lax.broadcasted_iota(jnp.int32, (n, n), 1)
    work = jnp.concatenate([gram, jnp.where(row == col, 1.0, 0.0).astype(F32)], axis=1)
    rows = lax.broadcasted_iota(jnp.int32, (n, 1), 0)
    out = []
    for k in range(n):
        pivot = work[k : k + 1, k : k + 1]
        scale = lax.rsqrt(pivot)
        scale = scale * (1.5 - 0.5 * pivot * scale * scale)
        scaled = work[k : k + 1, :] * scale
        out.append(scaled[:, n:])
        if k < n - 1:
            column = jnp.where(rows > k, work[:, k : k + 1], 0.0) * scale
            work = work - column * scaled
    return jnp.concatenate(out, axis=0)


def kernel(
    a_hbm, c_hbm, e_hbm, b_hbm, upd_ref, right_ref,
    a_v, c_v, e_v, b_v, lt, xrec, rs1, zt, zx, rs2,
    rrec1, rrec2, chunk1, chunk2, zrec1, zrec2, sum1, sum2, gat1, gat2,
    zacc, stack, left_abs, basis_blk,
    load, xr1, xr2, rr, zr, gr1, gr2, send,
):
    g, d = lax.axis_index("grp"), lax.axis_index("dp")
    core = lax.rem(g, 2)
    other = 1 - core
    x = lax.div(d, 32) * 2 + lax.div(g, 2)
    y = lax.rem(lax.div(d, 8), 4)
    z = lax.rem(d, 8)

    def at(dx, dy, dz, c):
        xx, yy, zz = lax.rem(x + dx, 4), lax.rem(y + dy, 4), lax.rem(z + dz, 8)
        return (lax.rem(xx, 2) * 2 + c, (lax.div(xx, 2) * 4 + yy) * 8 + zz)

    def place(i):
        return lax.rem(x + OFF[i][0], 4) * 4 + lax.rem(y + OFF[i][1], 4)

    def columns(i):
        return pl.ds(pl.multiple_of(place(i) * 128, 128), 128)

    def remote(src, dst, s, r, device):
        return pltpu.make_async_remote_copy(
            src_ref=src, dst_ref=dst, send_sem=s, recv_sem=r, device_id=device, device_id_type=MESH
        )

    def took(ref, sem):
        pltpu.make_async_copy(ref, ref, sem).wait()

    barrier = pltpu.get_barrier_semaphore()
    pl.semaphore_signal(barrier, inc=1, device_id=at(0, 0, 0, other), device_id_type=MESH)
    for dx, dy in OFF[:15]:
        for c in (core, other):
            pl.semaphore_signal(barrier, inc=1, device_id=at(dx, dy, 0, c), device_id_type=MESH)
    for dz in ZOFF:
        pl.semaphore_signal(barrier, inc=1, device_id=at(0, 0, dz, core), device_id_type=MESH)

    get_b = pltpu.make_async_copy(b_hbm, b_v, load.at[0])
    get_c = pltpu.make_async_copy(c_hbm, c_v, load.at[1])
    get_a = pltpu.make_async_copy(a_hbm, a_v, load.at[2])
    get_b.start()
    get_c.start()
    get_a.start()
    get_e = []
    for i in range(16):
        rows = pl.ds(pl.multiple_of(place(i) * 128, 128), 128)
        get_e.append(pltpu.make_async_copy(e_hbm.at[rows], e_v.at[pl.ds(128 * i, 128)], load.at[3 + i]))
        get_e[i].start()

    def a_pair(p):
        return jnp.concatenate([a_v[:, columns(2 * p)], a_v[:, columns(2 * p + 1)]], axis=1)

    get_b.wait()
    b2 = split2(b_v[...])
    get_c.wait()
    p2 = split2(fold(nt(b2, c_v[...])))
    get_a.wait()

    def push1(p):
        pair = pl.ds(2 * p, 2)
        took(xrec.at[pair], xr1.at[p])
        for i in (2 * p, 2 * p + 1):
            rs1[i] = lt[core, i] + xrec[i]
            if i < 15:
                dx, dy = OFF[i]
                remote(rs1.at[i], rrec1.at[i], send.at[1], rr.at[0], at(dx, dy, 0, core)).start()

    for p in range(8):
        get_e[2 * p].wait()
        get_e[2 * p + 1].wait()
        part = fold(nt(b2, e_v[256 * p : 256 * p + 256, :]) + nn(p2, a_pair(p)))
        for h in range(2):
            for k in range(2):
                lt[h, 2 * p + k] = part[16 * h : 16 * h + 16, 128 * k : 128 * k + 128]
        if p == 0:
            pl.semaphore_wait(barrier, 38)
        pair = pl.ds(2 * p, 2)
        remote(lt.at[other, pair], xrec.at[pair], send.at[0], xr1.at[p], at(0, 0, 0, other)).start()
        if p >= 1:
            push1(p - 1)
    push1(7)

    def finish(n, own, rrec, chunk, zrec, total, gat, gr):
        took(rrec, rr.at[n])
        acc = own
        for i in range(15):
            acc = acc + rrec[i]
        chunk[...] = acc
        for dz in ZOFF:
            remote(chunk, zrec.at[z], send.at[2 + 4 * n], zr.at[n], at(0, 0, dz, core)).start()
        zrec[z] = acc
        took(zrec.at[pl.ds(0, 7)], zr.at[n])
        acc = zrec[0]
        for k in range(1, 8):
            acc = acc + zrec[k]
        total[...] = acc
        for i in range(15):
            dx, dy = OFF[i]
            for c in (core, other):
                slot = NEG[i]
                remote(
                    total, gat.at[slot, core], send.at[3 + 4 * n], gr.at[slot // 2], at(dx, dy, 0, c)
                ).start()
        remote(total, gat.at[15, core], send.at[3 + 4 * n], gr.at[8], at(0, 0, 0, other)).start()
        gat[15, core] = acc

    def gathered(p, gat, gr):
        if p < 7:
            took(gat.at[pl.ds(2 * p, 2)], gr.at[p])
        else:
            took(gat.at[14], gr.at[7])
            took(gat.at[15, other], gr.at[8])
        return [gat[i].reshape(32, 128) for i in (2 * p, 2 * p + 1)]

    finish(0, rs1[15], rrec1, chunk1, zrec1, sum1, gat1, gr1)

    image = jnp.zeros((64, 512), F32)
    for p in range(7, -1, -1):
        pair = jnp.concatenate(gathered(p, gat1, gr1), axis=1)
        l2 = split2(pair)
        part = nn(l2, e_v[256 * p : 256 * p + 256, :])
        zacc[...] = part if p == 7 else zacc[...] + part
        image = image + nt(l2, a_pair(p))
    i2 = split2(fold(image))
    for j in range(4):
        cols = slice(512 * j, 512 * j + 512)
        part = fold(zacc[:, cols] + nn(i2, c_v[:, cols]))
        for h in range(2):
            for k in range(4):
                zt[h, 4 * j + k] = part[16 * h : 16 * h + 16, 128 * k : 128 * k + 128]
        quad = pl.ds(4 * j, 4)
        remote(zt.at[other, quad], zx.at[quad], send.at[4], xr2.at[j], at(0, 0, 0, other)).start()
    for j in range(4):
        quad = pl.ds(4 * j, 4)
        took(zx.at[quad], xr2.at[j])
        rs2[quad] = zt[core, quad] + zx[quad]
    for i in range(15):
        dx, dy = OFF[i]
        remote(rs2.at[place(i)], rrec2.at[i], send.at[5], rr.at[1], at(dx, dy, 0, core)).start()

    for i in range(16):
        block = gat1[i].reshape(32, 128)
        left_abs[place(i)] = block
        stack[:, columns(i)] = jnp.concatenate(split3(block), axis=0)
    products = nt(stack[...], stack[...])

    def piece(r, c):
        return products[32 * r : 32 * r + 32, 32 * c : 32 * c + 32]

    gram = piece(0, 0) + (piece(0, 1) + piece(1, 0)) + (piece(1, 1) + piece(0, 2) + piece(2, 0))
    inverse = left_stack(inverse_cholesky(gram))
    me = g * 64 + d
    basis_blk[...] = nn(inverse, right_stack(left_abs[lax.div(me, 16)])).T
    own_basis = left_stack(basis_blk[pl.ds(pl.multiple_of(lax.rem(me, 16) * 8, 8), 8), :])

    finish(1, rs2[place(15)], rrec2, chunk2, zrec2, sum2, gat2, gr2)

    for p in range(7, -1, -1):
        pair = jnp.concatenate(gathered(p, gat2, gr2), axis=1)
        right = nn(inverse, right_stack(pair))
        update = nn(own_basis, right_stack(right)).astype(BF16)
        for k in range(2):
            lanes = slice(128 * k, 128 * k + 128)
            right_ref[:, columns(2 * p + k)] = right[:, lanes]
            upd_ref[:, columns(2 * p + k)] = update[:, lanes]

    took(lt.at[0], send.at[0])
    took(zt.at[0], send.at[4])
    for n, rrec, zrec, gat in ((0, rrec1, zrec1, gat1), (1, rrec2, zrec2, gat2)):
        took(rrec, send.at[1 + 4 * n])
        took(zrec.at[pl.ds(0, 7)], send.at[2 + 4 * n])
        took(gat.at[pl.ds(0, 15)], send.at[3 + 4 * n])
        took(gat.at[15, 0], send.at[3 + 4 * n])


def local(activations, cotangent, error_buffer, basis_start):
    vm = pltpu.VMEM
    dma = pltpu.SemaphoreType.DMA
    chunk = (16, 128)
    update, right = pl.pallas_call(
        kernel,
        out_shape=(jax.ShapeDtypeStruct((8, 2048), BF16), jax.ShapeDtypeStruct((32, 2048), F32)),
        in_specs=[pl.BlockSpec(memory_space=pl.ANY)] * 4,
        out_specs=[pl.BlockSpec(memory_space=pltpu.VMEM)] * 2,
        scratch_shapes=[
            vm((512, 2048), BF16), vm((512, 2048), BF16), vm((2048, 2048), BF16), vm((32, 2048), F32),
            vm((2, 16) + chunk, F32), vm((16,) + chunk, F32), vm((16,) + chunk, F32),
            vm((2, 16) + chunk, F32), vm((16,) + chunk, F32), vm((16,) + chunk, F32),
            vm((15,) + chunk, F32), vm((15,) + chunk, F32), vm(chunk, F32), vm(chunk, F32),
            vm((8,) + chunk, F32), vm((8,) + chunk, F32), vm(chunk, F32), vm(chunk, F32),
            vm((16, 2) + chunk, F32), vm((16, 2) + chunk, F32),
            vm((64, 2048), F32), vm((96, 2048), BF16), vm((16, 32, 128), F32), vm((128, 32), F32),
            dma((19,)), dma((8,)), dma((4,)), dma((2,)), dma((2,)), dma((9,)), dma((9,)), dma((8,)),
        ],
        compiler_params=pltpu.CompilerParams(
            collective_id=0, has_side_effects=True, vmem_limit_bytes=48 << 20
        ),
        name="powersgd",
    )(activations, cotangent, error_buffer, basis_start.T)
    return update, right.T


def solution(mesh):
    placed = (P(("grp", "dp"), None), P(("grp", "dp"), None), P(("grp", "dp"), None), P())
    return jax.shard_map(
        local, mesh=mesh, in_specs=placed, out_specs=(P(("grp", "dp"), None), P()), check_vma=False
    )
```

```python
import functools

import jax
import jax.numpy as jnp
from jax import lax
from jax.experimental import pallas as pl
from jax.experimental.pallas import tpu as pltpu
from jax.sharding import PartitionSpec as P

MESH = pl.DeviceIdType.MESH
F32, BF16 = jnp.float32, jnp.bfloat16


RING = [2, 1, 3, 0]
OFF = [(dx, dy) for dx in RING for dy in RING]
NEG = [OFF.index(((-dx) % 4, (-dy) % 4)) for dx, dy in OFF]
ZOFF = [4, 3, 5, 2, 6, 1, 7]
GROUPS = [(4, 8), (2, 4), (1, 2), (0, 1)]


def split2(x):
    hi = x.astype(BF16)
    return jnp.concatenate([hi, (x - hi.astype(F32)).astype(BF16)], axis=0)


def split3(x):
    hi = x.astype(BF16)
    rest = x - hi.astype(F32)
    mid = rest.astype(BF16)
    return hi, mid, (rest - mid.astype(F32)).astype(BF16)


def left_stack(x):
    hi, mid, low = split3(x)
    return jnp.concatenate([hi, hi, mid, mid, hi, low], axis=1)


def right_stack(x):
    hi, mid, low = split3(x)
    return jnp.concatenate([hi, mid, hi, mid, low, hi], axis=0)


def nn(a, b):
    return lax.dot_general(a, b, (((1,), (0,)), ((), ())), preferred_element_type=F32)


def nt(a, b):
    return lax.dot_general(a, b, (((1,), (1,)), ((), ())), preferred_element_type=F32)


def fold(x):
    half = x.shape[0] // 2
    return x[:half] + x[half:]


def inverse_cholesky(gram):
    n = gram.shape[0]
    row = lax.broadcasted_iota(jnp.int32, (n, n), 0)
    col = lax.broadcasted_iota(jnp.int32, (n, n), 1)
    work = jnp.concatenate([gram, jnp.where(row == col, 1.0, 0.0).astype(F32)], axis=1)
    rows = lax.broadcasted_iota(jnp.int32, (n, 1), 0)
    out = []
    for k in range(n):
        pivot = work[k : k + 1, k : k + 1]
        scale = lax.rsqrt(pivot)
        scale = scale * (1.5 - 0.5 * pivot * scale * scale)
        scaled = work[k : k + 1, :] * scale
        out.append(scaled[:, n:])
        if k < n - 1:
            column = jnp.where(rows > k, work[:, k : k + 1], 0.0) * scale
            work = work - column * scaled
    return jnp.concatenate(out, axis=0)


def kernel(
    a_hbm, c_hbm, e_hbm, b_hbm, upd_ref, right_ref,
    a_v, c_v, e_v, b_v, at_v, lt, zt,
    rrec1, rrec2, chunk1, chunk2, zrec1, zrec2, sum1, sum2, gat1, gat2,
    zacc, stack, left_abs, basis_blk,
    load, rr, zr, gr1, gr2, send,
):
    g, d = lax.axis_index("grp"), lax.axis_index("dp")
    core = lax.rem(g, 2)
    other = 1 - core
    x = lax.div(d, 32) * 2 + lax.div(g, 2)
    y = lax.rem(lax.div(d, 8), 4)
    z = lax.rem(d, 8)

    def at(dx, dy, dz, c):
        xx, yy, zz = lax.rem(x + dx, 4), lax.rem(y + dy, 4), lax.rem(z + dz, 8)
        return (lax.rem(xx, 2) * 2 + c, (lax.div(xx, 2) * 4 + yy) * 8 + zz)

    def step(k):
        return jnp.where(k < 2, 2 - k, lax.rem(k + 1, 4))

    def offset(i):
        return OFF[i] if isinstance(i, int) else (step(lax.div(i, 4)), step(lax.rem(i, 4)))

    def place(i):
        dx, dy = offset(i)
        return lax.rem(x + dx, 4) * 4 + lax.rem(y + dy, 4)

    def columns(i):
        return pl.ds(pl.multiple_of(place(i) * 128, 128), 128)

    def remote(src, dst, s, r, device):
        return pltpu.make_async_remote_copy(
            src_ref=src, dst_ref=dst, send_sem=s, recv_sem=r, device_id=device, device_id_type=MESH
        )

    def took(ref, sem):
        pltpu.make_async_copy(ref, ref, sem).wait()

    get_b = pltpu.make_async_copy(b_hbm, b_v, load.at[0])
    get_c = pltpu.make_async_copy(c_hbm, c_v, load.at[1])
    get_a = pltpu.make_async_copy(a_hbm, a_v, load.at[2])
    get_b.start()
    get_c.start()
    get_a.start()

    barrier = pltpu.get_barrier_semaphore()
    pl.semaphore_signal(barrier, inc=1, device_id=at(0, 0, 0, other), device_id_type=MESH)
    for dx, dy in OFF[:15]:
        for c in (core, other):
            pl.semaphore_signal(barrier, inc=1, device_id=at(dx, dy, 0, c), device_id_type=MESH)
    for dz in ZOFF:
        pl.semaphore_signal(barrier, inc=1, device_id=at(0, 0, dz, core), device_id_type=MESH)

    def get_e(i):
        rows = pl.ds(pl.multiple_of(place(i) * 128, 128), 128)
        return pltpu.make_async_copy(
            e_hbm.at[rows], e_v.at[pl.ds(pl.multiple_of(i * 128, 128), 128)], load.at[3 + i]
        )

    @pl.loop(0, 16)
    def _(i):
        get_e(i).start()

    def both(ref, rows, j):
        return jnp.concatenate([ref[rows, columns(2 * j)], ref[rows, columns(2 * j + 1)]], axis=1)

    def scatter(n, src, rrec, i):
        dx, dy = offset(i)
        for c in (core, other):
            if not isinstance(i, int) or i < 15:
                remote(src.at[c, i], rrec.at[core * 16 + i], send.at[3 * n], rr.at[n], at(dx, dy, 0, c)).start()
        if isinstance(i, int) and i == 15:
            remote(
                src.at[other, i], rrec.at[core * 16 + i], send.at[3 * n], rr.at[n], at(0, 0, 0, other)
            ).start()
            rrec[core * 16 + 15] = src[core, 15]

    every = slice(None)
    get_b.wait()
    b2 = split2(b_v[...]).T
    get_c.wait()
    p2 = split2(fold(nn(c_v[...], b2).T))
    get_a.wait()

    def first_pass(p):
        for k in range(4):
            get_e(4 * p + k).wait()
        rows = pl.ds(pl.multiple_of(p * 512, 512), 512)
        cols = jnp.concatenate([a_v[:, columns(4 * p + k)] for k in range(4)], axis=1)
        part = fold(nn(e_v[rows, :], b2).T + nn(p2, cols))
        for h in range(2):
            for k in range(4):
                lt[h, 4 * p + k] = part[16 * h : 16 * h + 16, 128 * k : 128 * k + 128]

    @pl.loop(0, 3)
    def _(p):
        first_pass(p)

    pl.semaphore_wait(barrier, 38)

    @pl.loop(0, 12)
    def _(i):
        scatter(0, lt, rrec1, i)

    first_pass(3)
    for i in range(12, 16):
        scatter(0, lt, rrec1, i)

    def finish(n, rrec, chunk, zrec, total, gat, gr, meanwhile):
        took(rrec.at[pl.ds(0, 31)], rr.at[n])
        acc = rrec[0]
        for i in range(1, 32):
            acc = acc + rrec[i]
        chunk[...] = acc
        for dz in ZOFF:
            remote(chunk, zrec.at[z], send.at[1 + 3 * n], zr.at[n], at(0, 0, dz, core)).start()
        zrec[z] = acc
        result = meanwhile()
        took(zrec.at[pl.ds(0, 7)], zr.at[n])
        acc = zrec[0]
        for k in range(1, 8):
            acc = acc + zrec[k]
        total[...] = acc
        for i in range(15):
            dx, dy = OFF[i]
            for c in (core, other):
                slot = NEG[i]
                remote(
                    total, gat.at[slot, core], send.at[2 + 3 * n], gr.at[slot // 2], at(dx, dy, 0, c)
                ).start()
        remote(total, gat.at[15, core], send.at[2 + 3 * n], gr.at[8], at(0, 0, 0, other)).start()
        gat[15, core] = acc
        return result

    def gathered(first, last, gat, gr):
        for p in range(first, last):
            if p < 7:
                took(gat.at[pl.ds(2 * p, 2)], gr.at[p])
            else:
                took(gat.at[14], gr.at[7])
                took(gat.at[15, other], gr.at[8])
        return jnp.concatenate([gat[i].reshape(32, 128) for i in range(2 * first, 2 * last)], axis=1)

    @pl.loop(0, 8)
    def _(p):
        at_v[pl.ds(pl.multiple_of(p * 256, 256), 256), :] = both(a_v, every, p).T

    finish(0, rrec1, chunk1, zrec1, sum1, gat1, gr1, lambda: None)

    image = None
    for first, last in GROUPS:
        rows = slice(256 * first, 256 * last)
        l2 = split2(gathered(first, last, gat1, gr1))
        part = nn(l2, at_v[rows, :])
        image = part if image is None else image + part
        if first == 0:
            break
        for j in range(4):
            cols = slice(512 * j, 512 * j + 512)
            part = nn(l2, e_v[rows, cols])
            zacc[:, cols] = part if last == 8 else zacc[:, cols] + part
    i2 = split2(fold(image))

    def second_pass(j):
        part = fold(both(zacc, every, j) + nn(l2, both(e_v, rows, j)) + nn(i2, both(c_v, every, j)))
        for h in range(2):
            for k in range(2):
                zt[h, 2 * j + k] = part[16 * h : 16 * h + 16, 128 * k : 128 * k + 128]
        scatter(1, zt, rrec2, 2 * j)
        scatter(1, zt, rrec2, 2 * j + 1)

    @pl.loop(0, 7)
    def _(j):
        second_pass(j)

    second_pass(7)

    for i in range(16):
        block = gat1[i].reshape(32, 128)
        left_abs[place(i)] = block
        stack[:, columns(i)] = jnp.concatenate(split3(block), axis=0)
    products = nt(stack[...], stack[...])

    def piece(r, c):
        return products[32 * r : 32 * r + 32, 32 * c : 32 * c + 32]

    gram = piece(0, 0) + (piece(0, 1) + piece(1, 0)) + (piece(1, 1) + piece(0, 2) + piece(2, 0))
    inverse = left_stack(inverse_cholesky(gram))

    def own_rows():
        me = g * 64 + d
        basis_blk[...] = nn(inverse, right_stack(left_abs[lax.div(me, 16)])).T
        return left_stack(basis_blk[pl.ds(pl.multiple_of(lax.rem(me, 16) * 8, 8), 8), :])

    own_basis = finish(1, rrec2, chunk2, zrec2, sum2, gat2, gr2, own_rows)

    for first, last in GROUPS:
        right = nn(inverse, right_stack(gathered(first, last, gat2, gr2)))
        update = nn(own_basis, right_stack(right)).astype(BF16)
        for i in range(2 * first, 2 * last):
            lanes = slice(128 * (i - 2 * first), 128 * (i - 2 * first) + 128)
            right_ref[:, columns(i)] = right[:, lanes]
            upd_ref[:, columns(i)] = update[:, lanes]

    for n, rrec, zrec, gat in ((0, rrec1, zrec1, gat1), (1, rrec2, zrec2, gat2)):
        took(rrec.at[pl.ds(0, 31)], send.at[3 * n])
        took(zrec.at[pl.ds(0, 7)], send.at[1 + 3 * n])
        took(gat.at[pl.ds(0, 15)], send.at[2 + 3 * n])
        took(gat.at[15, 0], send.at[2 + 3 * n])


def local(activations, cotangent, error_buffer, basis_start):
    vm = pltpu.VMEM
    dma = pltpu.SemaphoreType.DMA
    chunk = (16, 128)
    update, right = pl.pallas_call(
        kernel,
        out_shape=(jax.ShapeDtypeStruct((8, 2048), BF16), jax.ShapeDtypeStruct((32, 2048), F32)),
        in_specs=[pl.BlockSpec(memory_space=pltpu.HBM)] * 4,
        out_specs=[pl.BlockSpec(memory_space=pltpu.VMEM)] * 2,
        scratch_shapes=[
            vm((512, 2048), BF16), vm((512, 2048), BF16), vm((2048, 2048), BF16), vm((32, 2048), F32),
            vm((2048, 512), BF16), vm((2, 16) + chunk, F32), vm((2, 16) + chunk, F32),
            vm((32,) + chunk, F32), vm((32,) + chunk, F32), vm(chunk, F32), vm(chunk, F32),
            vm((8,) + chunk, F32), vm((8,) + chunk, F32), vm(chunk, F32), vm(chunk, F32),
            vm((16, 2) + chunk, F32), vm((16, 2) + chunk, F32),
            vm((64, 2048), F32), vm((96, 2048), BF16), vm((16, 32, 128), F32), vm((128, 32), F32),
            dma((19,)), dma((2,)), dma((2,)), dma((9,)), dma((9,)), dma((6,)),
        ],
        compiler_params=pltpu.CompilerParams(
            collective_id=0, has_side_effects=True, vmem_limit_bytes=56098816
        ),
        name="powersgd",
    )(activations, cotangent, error_buffer, basis_start.T)
    return update, right.T


def solution(mesh):
    placed = (P(("grp", "dp"), None), P(("grp", "dp"), None), P(("grp", "dp"), None), P())
    return jax.shard_map(
        local, mesh=mesh, in_specs=placed, out_specs=(P(("grp", "dp"), None), P()), check_vma=False
    )
```

```python
import functools

import jax
import jax.numpy as jnp
from jax import lax
from jax.experimental import pallas as pl
from jax.experimental.pallas import tpu as pltpu
from jax.sharding import PartitionSpec as P

MESH = pl.DeviceIdType.MESH
F32, BF16 = jnp.float32, jnp.bfloat16


RING = [2, 1, 3, 0]
OFF = [(dx, dy) for dx in RING for dy in RING]
NEG = [OFF.index(((-dx) % 4, (-dy) % 4)) for dx, dy in OFF]
ZOFF = [4, 3, 5, 2, 6, 1, 7]
HOPS = [min(dx, 4 - dx) + min(dy, 4 - dy) for dx, dy in OFF]
FAR = [i for i in range(16) if HOPS[i] > 2]
ORDER = sorted(range(15), key=lambda i: -HOPS[i])


def split2(x):
    hi = x.astype(BF16)
    return jnp.concatenate([hi, (x - hi.astype(F32)).astype(BF16)], axis=0)


def split3(x):
    hi = x.astype(BF16)
    rest = x - hi.astype(F32)
    mid = rest.astype(BF16)
    return hi, mid, (rest - mid.astype(F32)).astype(BF16)


def left_stack(x):
    hi, mid, low = split3(x)
    return jnp.concatenate([hi, hi, mid, mid, hi, low], axis=1)


def right_stack(x):
    hi, mid, low = split3(x)
    return jnp.concatenate([hi, mid, hi, mid, low, hi], axis=0)


def nn(a, b):
    return lax.dot_general(a, b, (((1,), (0,)), ((), ())), preferred_element_type=F32)


def nt(a, b):
    return lax.dot_general(a, b, (((1,), (1,)), ((), ())), preferred_element_type=F32)


def fold(x):
    half = x.shape[0] // 2
    return x[:half] + x[half:]


def inverse_cholesky(gram):
    n = gram.shape[0]
    row = lax.broadcasted_iota(jnp.int32, (n, n), 0)
    col = lax.broadcasted_iota(jnp.int32, (n, n), 1)
    work = jnp.concatenate([gram, jnp.where(row == col, 1.0, 0.0).astype(F32)], axis=1)
    rows = lax.broadcasted_iota(jnp.int32, (n, 1), 0)
    out = []
    for k in range(n):
        pivot = work[k : k + 1, k : k + 1]
        scale = lax.rsqrt(pivot)
        scale = scale * (1.5 - 0.5 * pivot * scale * scale)
        scaled = work[k : k + 1, :] * scale
        out.append(scaled[:, n:])
        if k < n - 1:
            column = jnp.where(rows > k, work[:, k : k + 1], 0.0) * scale
            work = work - column * scaled
    return jnp.concatenate(out, axis=0)


def kernel(
    a_hbm, c_hbm, e_hbm, b_hbm, upd_ref, right_ref,
    a_v, c_v, e_v, b_v, at_v, lt, zt,
    rrec1, rrec2, chunk1, chunk2, zrec1, zrec2, sum1, sum2, gat1, gat2,
    zacc, stack, left_abs, basis_blk,
    load, rr, zr, gr1, gr2, send,
):
    g, d = lax.axis_index("grp"), lax.axis_index("dp")
    core = lax.rem(g, 2)
    other = 1 - core
    x = lax.div(d, 32) * 2 + lax.div(g, 2)
    y = lax.rem(lax.div(d, 8), 4)
    z = lax.rem(d, 8)

    def at(dx, dy, dz, c):
        xx, yy, zz = lax.rem(x + dx, 4), lax.rem(y + dy, 4), lax.rem(z + dz, 8)
        return (lax.rem(xx, 2) * 2 + c, (lax.div(xx, 2) * 4 + yy) * 8 + zz)

    def step(k):
        return jnp.where(k < 2, 2 - k, lax.rem(k + 1, 4))

    def offset(i):
        return OFF[i] if isinstance(i, int) else (step(lax.div(i, 4)), step(lax.rem(i, 4)))

    def place(i):
        dx, dy = offset(i)
        return lax.rem(x + dx, 4) * 4 + lax.rem(y + dy, 4)

    def columns(i):
        return pl.ds(pl.multiple_of(place(i) * 128, 128), 128)

    def remote(src, dst, s, r, device):
        return pltpu.make_async_remote_copy(
            src_ref=src, dst_ref=dst, send_sem=s, recv_sem=r, device_id=device, device_id_type=MESH
        )

    def took(ref, sem):
        pltpu.make_async_copy(ref, ref, sem).wait()

    get_b = pltpu.make_async_copy(b_hbm, b_v, load.at[0])
    get_c = pltpu.make_async_copy(c_hbm, c_v, load.at[1])
    get_a = pltpu.make_async_copy(a_hbm, a_v, load.at[2])
    get_b.start()
    get_c.start()
    get_a.start()

    barrier = pltpu.get_barrier_semaphore()
    pl.semaphore_signal(barrier, inc=1, device_id=at(0, 0, 0, other), device_id_type=MESH)
    for dx, dy in OFF[:15]:
        for c in (core, other):
            pl.semaphore_signal(barrier, inc=1, device_id=at(dx, dy, 0, c), device_id_type=MESH)
    for dz in ZOFF:
        pl.semaphore_signal(barrier, inc=1, device_id=at(0, 0, dz, core), device_id_type=MESH)

    def get_e(i):
        rows = pl.ds(pl.multiple_of(place(i) * 128, 128), 128)
        return pltpu.make_async_copy(
            e_hbm.at[rows], e_v.at[pl.ds(pl.multiple_of(i * 128, 128), 128)], load.at[3 + i]
        )

    @pl.loop(0, 16)
    def _(i):
        get_e(i).start()

    def both(ref, rows, j):
        return jnp.concatenate([ref[rows, columns(2 * j)], ref[rows, columns(2 * j + 1)]], axis=1)

    def scatter(n, src, rrec, i):
        dx, dy = offset(i)
        for c in (core, other):
            if not isinstance(i, int) or i < 15:
                remote(src.at[c, i], rrec.at[core * 16 + i], send.at[3 * n], rr.at[n], at(dx, dy, 0, c)).start()
        if isinstance(i, int) and i == 15:
            remote(
                src.at[other, i], rrec.at[core * 16 + i], send.at[3 * n], rr.at[n], at(0, 0, 0, other)
            ).start()
            rrec[core * 16 + 15] = src[core, 15]

    every = slice(None)
    get_b.wait()
    b2 = split2(b_v[...]).T
    get_c.wait()
    p2 = split2(fold(nn(c_v[...], b2).T))
    get_a.wait()

    def first_pass(p):
        for k in range(4):
            get_e(4 * p + k).wait()
        rows = pl.ds(pl.multiple_of(p * 512, 512), 512)
        cols = jnp.concatenate([a_v[:, columns(4 * p + k)] for k in range(4)], axis=1)
        part = fold(nn(e_v[rows, :], b2).T + nn(p2, cols))
        for h in range(2):
            for k in range(4):
                lt[h, 4 * p + k] = part[16 * h : 16 * h + 16, 128 * k : 128 * k + 128]

    @pl.loop(0, 3)
    def _(p):
        first_pass(p)

    pl.semaphore_wait(barrier, 38)

    @pl.loop(0, 12)
    def _(i):
        scatter(0, lt, rrec1, i)

    first_pass(3)
    for i in range(12, 16):
        scatter(0, lt, rrec1, i)

    def finish(n, rrec, chunk, zrec, total, gat, gr, meanwhile):
        took(rrec.at[pl.ds(0, 31)], rr.at[n])
        acc = rrec[0]
        for i in range(1, 32):
            acc = acc + rrec[i]
        chunk[...] = acc
        for dz in ZOFF:
            remote(chunk, zrec.at[z], send.at[1 + 3 * n], zr.at[n], at(0, 0, dz, core)).start()
        zrec[z] = acc
        result = meanwhile()
        took(zrec.at[pl.ds(0, 7)], zr.at[n])
        acc = zrec[0]
        for k in range(1, 8):
            acc = acc + zrec[k]
        total[...] = acc
        for i in ORDER:
            dx, dy = OFF[i]
            slot = NEG[i]
            sem = gr.at[0 if slot in FAR else 1 if slot > 8 else 2]
            remote(total, gat.at[core, slot], send.at[2 + 3 * n], sem, at(dx, dy, 0, core)).start()
        for i in ORDER[:5]:
            dx, dy = OFF[i]
            remote(
                total, gat.at[core, NEG[i]], send.at[2 + 3 * n], gr.at[0], at(dx, dy, 0, other)
            ).start()
        remote(total, gat.at[core, 15], send.at[2 + 3 * n], gr.at[3], at(0, 0, 0, other)).start()
        gat[core, 15] = acc

        took(gat.at[core, pl.ds(9, 6)], gr.at[1])
        hand_on(gat, pl.ds(9, 6), 6 + n, gr.at[4])
        took(gat.at[core, pl.ds(3, 4)], gr.at[2])
        hand_on(gat, pl.ds(5, 3), 6 + n, gr.at[5])
        hand_on(gat, pl.ds(3, 1), 6 + n, gr.at[5])
        return result

    def hand_on(gat, blocks, s, r):
        part = gat.at[core, blocks]
        remote(part, part, send.at[s], r, at(0, 0, 0, other)).start()

    def gathered(first, last, gat):
        return jnp.concatenate(
            [jnp.concatenate([gat[0, i], gat[1, i]], axis=0) for i in range(first, last)], axis=1
        )

    def near_blocks(gat, gr):
        took(gat.at[other, pl.ds(9, 6)], gr.at[4])
        took(gat.at[other, 15], gr.at[3])

    def far_blocks(gat, gr):
        took(gat.at[0, pl.ds(0, 10)], gr.at[0])

    def last_blocks(gat, gr):
        took(gat.at[other, pl.ds(3, 4)], gr.at[5])

    @pl.loop(0, 8)
    def _(p):
        at_v[pl.ds(pl.multiple_of(p * 256, 256), 256), :] = both(a_v, every, p).T

    finish(0, rrec1, chunk1, zrec1, sum1, gat1, gr1, lambda: None)

    def accumulate(first, last, new):
        rows = slice(128 * first, 128 * last)
        l2 = split2(gathered(first, last, gat1))
        for j in range(4):
            cols = slice(512 * j, 512 * j + 512)
            part = nn(l2, e_v[rows, cols])
            zacc[:, cols] = part if new else zacc[:, cols] + part
        return nn(l2, at_v[rows, :])

    near_blocks(gat1, gr1)
    image = accumulate(10, 16, True)
    far_blocks(gat1, gr1)
    image = image + accumulate(8, 10, False) + accumulate(0, 2, False)
    last_blocks(gat1, gr1)
    rows = slice(256, 1024)
    l2 = split2(gathered(2, 8, gat1))
    image = image + nn(l2, at_v[rows, :])
    i2 = split2(fold(image))

    def second_pass(j):
        part = fold(both(zacc, every, j) + nn(l2, both(e_v, rows, j)) + nn(i2, both(c_v, every, j)))
        for h in range(2):
            for k in range(2):
                zt[h, 2 * j + k] = part[16 * h : 16 * h + 16, 128 * k : 128 * k + 128]
        scatter(1, zt, rrec2, 2 * j)
        scatter(1, zt, rrec2, 2 * j + 1)

    @pl.loop(0, 7)
    def _(j):
        second_pass(j)

    second_pass(7)

    for i in range(16):
        block = gathered(i, i + 1, gat1)
        left_abs[place(i)] = block
        stack[:, columns(i)] = jnp.concatenate(split3(block), axis=0)
    products = nt(stack[...], stack[...])

    def piece(r, c):
        return products[32 * r : 32 * r + 32, 32 * c : 32 * c + 32]

    gram = piece(0, 0) + (piece(0, 1) + piece(1, 0)) + (piece(1, 1) + piece(0, 2) + piece(2, 0))
    inverse = inverse_cholesky(gram)

    def factors():
        me = g * 64 + d
        basis_blk[...] = nn(left_stack(inverse), right_stack(left_abs[lax.div(me, 16)])).T
        own = left_stack(basis_blk[pl.ds(pl.multiple_of(lax.rem(me, 16) * 8, 8), 8), :])
        return left_stack(jnp.concatenate([inverse, nn(own, right_stack(inverse))], axis=0))

    both_factors = finish(1, rrec2, chunk2, zrec2, sum2, gat2, gr2, factors)
    near_blocks(gat2, gr2)
    far_blocks(gat2, gr2)
    last_blocks(gat2, gr2)
    for q in range(4):
        result = nn(both_factors, right_stack(gathered(4 * q, 4 * q + 4, gat2)))
        update = result[32:].astype(BF16)
        for k in range(4):
            lanes = slice(128 * k, 128 * k + 128)
            right_ref[:, columns(4 * q + k)] = result[:32, lanes]
            upd_ref[:, columns(4 * q + k)] = update[:, lanes]

    for n, rrec, zrec, gat in ((0, rrec1, zrec1, gat1), (1, rrec2, zrec2, gat2)):
        took(rrec.at[pl.ds(0, 31)], send.at[3 * n])
        took(zrec.at[pl.ds(0, 7)], send.at[1 + 3 * n])
        took(gat.at[0], send.at[2 + 3 * n])
        took(gat.at[0, pl.ds(0, 5)], send.at[2 + 3 * n])
        took(gat.at[0, pl.ds(0, 10)], send.at[6 + n])


def local(activations, cotangent, error_buffer, basis_start):
    vm = pltpu.VMEM
    dma = pltpu.SemaphoreType.DMA
    chunk = (16, 128)
    update, right = pl.pallas_call(
        kernel,
        out_shape=(jax.ShapeDtypeStruct((8, 2048), BF16), jax.ShapeDtypeStruct((32, 2048), F32)),
        in_specs=[pl.BlockSpec(memory_space=pltpu.HBM)] * 4,
        out_specs=[pl.BlockSpec(memory_space=pltpu.VMEM)] * 2,
        scratch_shapes=[
            vm((512, 2048), BF16), vm((512, 2048), BF16), vm((2048, 2048), BF16), vm((32, 2048), F32),
            vm((2048, 512), BF16), vm((2, 16) + chunk, F32), vm((2, 16) + chunk, F32),
            vm((32,) + chunk, F32), vm((32,) + chunk, F32), vm(chunk, F32), vm(chunk, F32),
            vm((8,) + chunk, F32), vm((8,) + chunk, F32), vm(chunk, F32), vm(chunk, F32),
            vm((2, 16) + chunk, F32), vm((2, 16) + chunk, F32),
            vm((64, 2048), F32), vm((96, 2048), BF16), vm((16, 32, 128), F32), vm((128, 32), F32),
            dma((19,)), dma((2,)), dma((2,)), dma((6,)), dma((6,)), dma((8,)),
        ],
        compiler_params=pltpu.CompilerParams(
            collective_id=0, has_side_effects=True, vmem_limit_bytes=56098816
        ),
        name="powersgd",
    )(activations, cotangent, error_buffer, basis_start.T)
    return update, right.T


def solution(mesh):
    placed = (P(("grp", "dp"), None), P(("grp", "dp"), None), P(("grp", "dp"), None), P())
    return jax.shard_map(
        local, mesh=mesh, in_specs=placed, out_specs=(P(("grp", "dp"), None), P()), check_vma=False
    )
```

```python
import functools

import jax
import jax.numpy as jnp
from jax import lax
from jax.experimental import pallas as pl
from jax.experimental.pallas import tpu as pltpu
from jax.sharding import PartitionSpec as P

MESH = pl.DeviceIdType.MESH
F32, BF16 = jnp.float32, jnp.bfloat16


RING = [2, 1, 3, 0]
OFF = [(dx, dy) for dx in RING for dy in RING]
NEG = [OFF.index(((-dx) % 4, (-dy) % 4)) for dx, dy in OFF]
ZOFF = [4, 3, 5, 2, 6, 1, 7]
HOPS = [min(dx, 4 - dx) + min(dy, 4 - dy) for dx, dy in OFF]
FAR = [i for i in range(16) if HOPS[i] > 2]
ORDER = sorted(range(15), key=lambda i: -HOPS[i])


def split2(x):
    hi = x.astype(BF16)
    return jnp.concatenate([hi, (x - hi.astype(F32)).astype(BF16)], axis=0)


def split3(x):
    hi = x.astype(BF16)
    rest = x - hi.astype(F32)
    mid = rest.astype(BF16)
    return hi, mid, (rest - mid.astype(F32)).astype(BF16)


def left_stack(x):
    hi, mid, low = split3(x)
    return jnp.concatenate([hi, hi, mid, mid, hi, low], axis=1)


def right_stack(x):
    hi, mid, low = split3(x)
    return jnp.concatenate([hi, mid, hi, mid, low, hi], axis=0)


def nn(a, b):
    return lax.dot_general(a, b, (((1,), (0,)), ((), ())), preferred_element_type=F32)


def nt(a, b):
    return lax.dot_general(a, b, (((1,), (1,)), ((), ())), preferred_element_type=F32)


def fold(x):
    half = x.shape[0] // 2
    return x[:half] + x[half:]


def inverse_cholesky(gram):
    n = gram.shape[0]
    row = lax.broadcasted_iota(jnp.int32, (n, n), 0)
    col = lax.broadcasted_iota(jnp.int32, (n, n), 1)
    work = jnp.concatenate([gram, jnp.where(row == col, 1.0, 0.0).astype(F32)], axis=1)
    rows = lax.broadcasted_iota(jnp.int32, (n, 1), 0)
    out = []
    for k in range(n):
        pivot = work[k : k + 1, k : k + 1]
        scale = lax.rsqrt(pivot)
        scale = scale * (1.5 - 0.5 * pivot * scale * scale)
        scaled = work[k : k + 1, :] * scale
        out.append(scaled[:, n:])
        if k < n - 1:
            column = jnp.where(rows > k, work[:, k : k + 1], 0.0) * scale
            work = work - column * scaled
    return jnp.concatenate(out, axis=0)


def kernel(
    a_hbm, c_hbm, e_hbm, b_hbm, upd_ref, right_ref,
    a_v, c_v, e_v, b_v, at_v, lt, zt,
    rrec1, rrec2, chunk1, chunk2, zrec1, zrec2, sum1, sum2, gat1, gat2,
    zacc, stack, left_abs, basis_blk,
    load, rr, zr, gr1, gr2, send,
):
    g, d = lax.axis_index("grp"), lax.axis_index("dp")
    core = lax.rem(g, 2)
    other = 1 - core
    x = lax.div(d, 32) * 2 + lax.div(g, 2)
    y = lax.rem(lax.div(d, 8), 4)
    z = lax.rem(d, 8)

    def at(dx, dy, dz, c):
        xx, yy, zz = lax.rem(x + dx, 4), lax.rem(y + dy, 4), lax.rem(z + dz, 8)
        return (lax.rem(xx, 2) * 2 + c, (lax.div(xx, 2) * 4 + yy) * 8 + zz)

    def step(k):
        return jnp.where(k < 2, 2 - k, lax.rem(k + 1, 4))

    def offset(i):
        return OFF[i] if isinstance(i, int) else (step(lax.div(i, 4)), step(lax.rem(i, 4)))

    def place(i):
        dx, dy = offset(i)
        return lax.rem(x + dx, 4) * 4 + lax.rem(y + dy, 4)

    def columns(i):
        return pl.ds(pl.multiple_of(place(i) * 128, 128), 128)

    def remote(src, dst, s, r, device):
        return pltpu.make_async_remote_copy(
            src_ref=src, dst_ref=dst, send_sem=s, recv_sem=r, device_id=device, device_id_type=MESH
        )

    def took(ref, sem):
        pltpu.make_async_copy(ref, ref, sem).wait()

    get_b = pltpu.make_async_copy(b_hbm, b_v, load.at[0])
    get_c = pltpu.make_async_copy(c_hbm, c_v, load.at[1])
    get_a = pltpu.make_async_copy(a_hbm, a_v, load.at[2])
    get_b.start()
    get_c.start()
    get_a.start()

    barrier = pltpu.get_barrier_semaphore()
    pl.semaphore_signal(barrier, inc=1, device_id=at(0, 0, 0, other), device_id_type=MESH)
    for dx, dy in OFF[:15]:
        for c in (core, other):
            pl.semaphore_signal(barrier, inc=1, device_id=at(dx, dy, 0, c), device_id_type=MESH)
    for dz in ZOFF:
        pl.semaphore_signal(barrier, inc=1, device_id=at(0, 0, dz, core), device_id_type=MESH)

    def get_e(i):
        rows = pl.ds(pl.multiple_of(place(i) * 128, 128), 128)
        return pltpu.make_async_copy(
            e_hbm.at[rows], e_v.at[pl.ds(pl.multiple_of(i * 128, 128), 128)], load.at[3 + i]
        )

    @pl.loop(0, 16)
    def _(i):
        get_e(i).start()

    def both(ref, rows, j):
        return jnp.concatenate([ref[rows, columns(2 * j)], ref[rows, columns(2 * j + 1)]], axis=1)

    def scatter(n, src, rrec, i):
        dx, dy = offset(i)
        for c in (core, other):
            if not isinstance(i, int) or i < 15:
                remote(src.at[c, i], rrec.at[core * 16 + i], send.at[3 * n], rr.at[n], at(dx, dy, 0, c)).start()
        if isinstance(i, int) and i == 15:
            remote(
                src.at[other, i], rrec.at[core * 16 + i], send.at[3 * n], rr.at[n], at(0, 0, 0, other)
            ).start()
            rrec[core * 16 + 15] = src[core, 15]

    every = slice(None)
    get_b.wait()
    b2 = split2(b_v[...]).T
    get_c.wait()
    p2 = split2(fold(nn(c_v[...], b2).T))
    get_a.wait()

    def first_pass(p):
        for k in range(4):
            get_e(4 * p + k).wait()
        rows = pl.ds(pl.multiple_of(p * 512, 512), 512)
        cols = jnp.concatenate([a_v[:, columns(4 * p + k)] for k in range(4)], axis=1)
        part = fold(nn(e_v[rows, :], b2).T + nn(p2, cols))
        for h in range(2):
            for k in range(4):
                lt[h, 4 * p + k] = part[16 * h : 16 * h + 16, 128 * k : 128 * k + 128]

    @pl.loop(0, 2)
    def _(p):
        first_pass(p)

    pl.semaphore_wait(barrier, 38)

    @pl.loop(0, 8)
    def _(i):
        scatter(0, lt, rrec1, i)

    first_pass(2)

    @pl.loop(8, 12)
    def _(i):
        scatter(0, lt, rrec1, i)

    first_pass(3)
    for i in range(12, 16):
        scatter(0, lt, rrec1, i)

    def finish(n, rrec, chunk, zrec, total, gat, gr, meanwhile):
        took(rrec.at[pl.ds(0, 31)], rr.at[n])
        acc = rrec[0]
        for i in range(1, 32):
            acc = acc + rrec[i]
        chunk[...] = acc
        for dz in ZOFF:
            remote(chunk, zrec.at[z], send.at[1 + 3 * n], zr.at[n], at(0, 0, dz, core)).start()
        zrec[z] = acc
        result = meanwhile()
        took(zrec.at[pl.ds(0, 7)], zr.at[n])
        acc = zrec[0]
        for k in range(1, 8):
            acc = acc + zrec[k]
        total[...] = acc
        for i in ORDER:
            dx, dy = OFF[i]
            slot = NEG[i]
            sem = gr.at[0 if slot in FAR else 1 if slot > 8 else 2]
            remote(total, gat.at[core, slot], send.at[2 + 3 * n], sem, at(dx, dy, 0, core)).start()
        for i in ORDER[:5]:
            dx, dy = OFF[i]
            remote(
                total, gat.at[core, NEG[i]], send.at[2 + 3 * n], gr.at[0], at(dx, dy, 0, other)
            ).start()
        remote(total, gat.at[core, 15], send.at[2 + 3 * n], gr.at[3], at(0, 0, 0, other)).start()
        gat[core, 15] = acc

        took(gat.at[core, pl.ds(9, 6)], gr.at[1])
        hand_on(gat, pl.ds(9, 6), 6 + n, gr.at[4])
        took(gat.at[core, pl.ds(3, 4)], gr.at[2])
        hand_on(gat, pl.ds(5, 3), 6 + n, gr.at[5])
        hand_on(gat, pl.ds(3, 1), 6 + n, gr.at[5])
        return result

    def hand_on(gat, blocks, s, r):
        part = gat.at[core, blocks]
        remote(part, part, send.at[s], r, at(0, 0, 0, other)).start()

    def gathered(first, last, gat):
        return jnp.concatenate(
            [jnp.concatenate([gat[0, i], gat[1, i]], axis=0) for i in range(first, last)], axis=1
        )

    def near_blocks(gat, gr):
        took(gat.at[other, pl.ds(9, 6)], gr.at[4])
        took(gat.at[other, 15], gr.at[3])

    def far_blocks(gat, gr):
        took(gat.at[0, pl.ds(0, 10)], gr.at[0])

    def last_blocks(gat, gr):
        took(gat.at[other, pl.ds(3, 4)], gr.at[5])

    @pl.loop(0, 8)
    def _(p):
        at_v[pl.ds(pl.multiple_of(p * 256, 256), 256), :] = both(a_v, every, p).T

    finish(0, rrec1, chunk1, zrec1, sum1, gat1, gr1, lambda: None)

    def accumulate(first, last, new):
        rows = slice(128 * first, 128 * last)
        l2 = split2(gathered(first, last, gat1))
        for j in range(4):
            cols = slice(512 * j, 512 * j + 512)
            part = nn(l2, e_v[rows, cols])
            zacc[:, cols] = part if new else zacc[:, cols] + part
        return nn(l2, at_v[rows, :])

    near_blocks(gat1, gr1)
    image = accumulate(10, 16, True)
    far_blocks(gat1, gr1)
    image = image + accumulate(8, 10, False) + accumulate(0, 2, False)
    last_blocks(gat1, gr1)
    rows = slice(256, 1024)
    l2 = split2(gathered(2, 8, gat1))
    image = image + nn(l2, at_v[rows, :])
    i2 = split2(fold(image))

    def second_pass(j):
        part = fold(both(zacc, every, j) + nn(l2, both(e_v, rows, j)) + nn(i2, both(c_v, every, j)))
        for h in range(2):
            for k in range(2):
                zt[h, 2 * j + k] = part[16 * h : 16 * h + 16, 128 * k : 128 * k + 128]
        scatter(1, zt, rrec2, 2 * j)
        scatter(1, zt, rrec2, 2 * j + 1)

    @pl.loop(0, 7)
    def _(j):
        second_pass(j)

    second_pass(7)

    for i in range(16):
        block = gathered(i, i + 1, gat1)
        left_abs[place(i)] = block
        stack[:, columns(i)] = jnp.concatenate(split3(block), axis=0)
    products = nt(stack[...], stack[...])

    def piece(r, c):
        return products[32 * r : 32 * r + 32, 32 * c : 32 * c + 32]

    gram = piece(0, 0) + (piece(0, 1) + piece(1, 0)) + (piece(1, 1) + piece(0, 2) + piece(2, 0))
    inverse = inverse_cholesky(gram)

    def factors():
        me = g * 64 + d
        basis_blk[...] = nn(left_stack(inverse), right_stack(left_abs[lax.div(me, 16)])).T
        own = left_stack(basis_blk[pl.ds(pl.multiple_of(lax.rem(me, 16) * 8, 8), 8), :])
        return left_stack(jnp.concatenate([inverse, nn(own, right_stack(inverse))], axis=0))

    both_factors = finish(1, rrec2, chunk2, zrec2, sum2, gat2, gr2, factors)
    near_blocks(gat2, gr2)
    far_blocks(gat2, gr2)
    last_blocks(gat2, gr2)
    for q in range(4):
        result = nn(both_factors, right_stack(gathered(4 * q, 4 * q + 4, gat2)))
        update = result[32:].astype(BF16)
        for k in range(4):
            lanes = slice(128 * k, 128 * k + 128)
            right_ref[:, columns(4 * q + k)] = result[:32, lanes]
            upd_ref[:, columns(4 * q + k)] = update[:, lanes]

    for n, rrec, zrec, gat in ((0, rrec1, zrec1, gat1), (1, rrec2, zrec2, gat2)):
        took(rrec.at[pl.ds(0, 31)], send.at[3 * n])
        took(zrec.at[pl.ds(0, 7)], send.at[1 + 3 * n])
        took(gat.at[0], send.at[2 + 3 * n])
        took(gat.at[0, pl.ds(0, 5)], send.at[2 + 3 * n])
        took(gat.at[0, pl.ds(0, 10)], send.at[6 + n])


def local(activations, cotangent, error_buffer, basis_start):
    vm = pltpu.VMEM
    dma = pltpu.SemaphoreType.DMA
    chunk = (16, 128)
    update, right = pl.pallas_call(
        kernel,
        out_shape=(jax.ShapeDtypeStruct((8, 2048), BF16), jax.ShapeDtypeStruct((32, 2048), F32)),
        in_specs=[pl.BlockSpec(memory_space=pltpu.HBM)] * 4,
        out_specs=[pl.BlockSpec(memory_space=pltpu.VMEM)] * 2,
        scratch_shapes=[
            vm((512, 2048), BF16), vm((512, 2048), BF16), vm((2048, 2048), BF16), vm((32, 2048), F32),
            vm((2048, 512), BF16), vm((2, 16) + chunk, F32), vm((2, 16) + chunk, F32),
            vm((32,) + chunk, F32), vm((32,) + chunk, F32), vm(chunk, F32), vm(chunk, F32),
            vm((8,) + chunk, F32), vm((8,) + chunk, F32), vm(chunk, F32), vm(chunk, F32),
            vm((2, 16) + chunk, F32), vm((2, 16) + chunk, F32),
            vm((64, 2048), F32), vm((96, 2048), BF16), vm((16, 32, 128), F32), vm((128, 32), F32),
            dma((19,)), dma((2,)), dma((2,)), dma((6,)), dma((6,)), dma((8,)),
        ],
        compiler_params=pltpu.CompilerParams(
            collective_id=0, has_side_effects=True, vmem_limit_bytes=56098816
        ),
        name="powersgd",
    )(activations, cotangent, error_buffer, basis_start.T)
    return update, right.T


def solution(mesh):
    placed = (P(("grp", "dp"), None), P(("grp", "dp"), None), P(("grp", "dp"), None), P())
    return jax.shard_map(
        local, mesh=mesh, in_specs=placed, out_specs=(P(("grp", "dp"), None), P()), check_vma=False
    )
```

```python
import functools

import jax
import jax.numpy as jnp
from jax import lax
from jax.experimental import pallas as pl
from jax.experimental.pallas import tpu as pltpu
from jax.sharding import PartitionSpec as P

MESH = pl.DeviceIdType.MESH
F32, BF16 = jnp.float32, jnp.bfloat16


RING = [2, 1, 3, 0]
OFF = [(dx, dy) for dx in RING for dy in RING]
NEG = [OFF.index(((-dx) % 4, (-dy) % 4)) for dx, dy in OFF]
ZOFF = [4, 3, 5, 2, 6, 1, 7]
HOPS = [min(dx, 4 - dx) + min(dy, 4 - dy) for dx, dy in OFF]
FAR = [i for i in range(16) if HOPS[i] > 2]
ORDER = sorted(range(15), key=lambda i: -HOPS[i])


def split2(x):
    hi = x.astype(BF16)
    return jnp.concatenate([hi, (x - hi.astype(F32)).astype(BF16)], axis=0)


def split3(x):
    hi = x.astype(BF16)
    rest = x - hi.astype(F32)
    mid = rest.astype(BF16)
    return hi, mid, (rest - mid.astype(F32)).astype(BF16)


def left_stack(x):
    hi, mid, low = split3(x)
    return jnp.concatenate([hi, hi, mid, mid, hi, low], axis=1)


def right_stack(x):
    hi, mid, low = split3(x)
    return jnp.concatenate([hi, mid, hi, mid, low, hi], axis=0)


def nn(a, b):
    return lax.dot_general(a, b, (((1,), (0,)), ((), ())), preferred_element_type=F32)


def nt(a, b):
    return lax.dot_general(a, b, (((1,), (1,)), ((), ())), preferred_element_type=F32)


def fold(x):
    half = x.shape[0] // 2
    return x[:half] + x[half:]


def inverse_cholesky(gram):
    n = gram.shape[0]
    row = lax.broadcasted_iota(jnp.int32, (n, n), 0)
    col = lax.broadcasted_iota(jnp.int32, (n, n), 1)
    work = jnp.concatenate([gram, jnp.where(row == col, 1.0, 0.0).astype(F32)], axis=1)
    rows = lax.broadcasted_iota(jnp.int32, (n, 1), 0)
    out = []
    for k in range(n):
        pivot = work[k : k + 1, k : k + 1]
        scale = lax.rsqrt(pivot)
        scale = scale * (1.5 - 0.5 * pivot * scale * scale)
        scaled = work[k : k + 1, :] * scale
        out.append(scaled[:, n:])
        if k < n - 1:
            column = jnp.where(rows > k, work[:, k : k + 1], 0.0) * scale
            work = work - column * scaled
    return jnp.concatenate(out, axis=0)


def kernel(
    a_hbm, c_hbm, e_hbm, b_hbm, upd_ref, right_ref,
    a_v, c_v, e_v, b_v, at_v, lt, zt,
    rrec1, rrec2, chunk1, chunk2, zrec1, zrec2, sum1, sum2, gat1, gat2,
    zacc, stack, left_abs, basis_blk,
    load, rr, zr, gr1, gr2, send,
):
    g, d = lax.axis_index("grp"), lax.axis_index("dp")
    core = lax.rem(g, 2)
    other = 1 - core
    x = lax.div(d, 32) * 2 + lax.div(g, 2)
    y = lax.rem(lax.div(d, 8), 4)
    z = lax.rem(d, 8)

    def at(dx, dy, dz, c):
        xx, yy, zz = lax.rem(x + dx, 4), lax.rem(y + dy, 4), lax.rem(z + dz, 8)
        return (lax.rem(xx, 2) * 2 + c, (lax.div(xx, 2) * 4 + yy) * 8 + zz)

    def step(k):
        return jnp.where(k < 2, 2 - k, lax.rem(k + 1, 4))

    def offset(i):
        return OFF[i] if isinstance(i, int) else (step(lax.div(i, 4)), step(lax.rem(i, 4)))

    def place(i):
        dx, dy = offset(i)
        return lax.rem(x + dx, 4) * 4 + lax.rem(y + dy, 4)

    def columns(i):
        return pl.ds(pl.multiple_of(place(i) * 128, 128), 128)

    def remote(src, dst, s, r, device):
        return pltpu.make_async_remote_copy(
            src_ref=src, dst_ref=dst, send_sem=s, recv_sem=r, device_id=device, device_id_type=MESH
        )

    def took(ref, sem):
        pltpu.make_async_copy(ref, ref, sem).wait()

    get_b = pltpu.make_async_copy(b_hbm, b_v, load.at[0])
    get_c = pltpu.make_async_copy(c_hbm, c_v, load.at[1])
    get_a = pltpu.make_async_copy(a_hbm, a_v, load.at[2])
    get_b.start()
    get_c.start()
    get_a.start()

    barrier = pltpu.get_barrier_semaphore()
    pl.semaphore_signal(barrier, inc=1, device_id=at(0, 0, 0, other), device_id_type=MESH)
    for dx, dy in OFF[:15]:
        for c in (core, other):
            pl.semaphore_signal(barrier, inc=1, device_id=at(dx, dy, 0, c), device_id_type=MESH)
    for dz in ZOFF:
        pl.semaphore_signal(barrier, inc=1, device_id=at(0, 0, dz, core), device_id_type=MESH)

    def get_e(i):
        rows = pl.ds(pl.multiple_of(place(i) * 128, 128), 128)
        return pltpu.make_async_copy(
            e_hbm.at[rows], e_v.at[pl.ds(pl.multiple_of(i * 128, 128), 128)], load.at[3 + i]
        )

    @pl.loop(0, 16)
    def _(i):
        get_e(i).start()

    def both(ref, rows, j):
        return jnp.concatenate([ref[rows, columns(2 * j)], ref[rows, columns(2 * j + 1)]], axis=1)

    def scatter(n, src, rrec, i):
        dx, dy = offset(i)
        for c in (core, other):
            if not isinstance(i, int) or i < 15:
                remote(src.at[c, i], rrec.at[core * 16 + i], send.at[3 * n], rr.at[n], at(dx, dy, 0, c)).start()
        if isinstance(i, int) and i == 15:
            remote(
                src.at[other, i], rrec.at[core * 16 + i], send.at[3 * n], rr.at[n], at(0, 0, 0, other)
            ).start()
            rrec[core * 16 + 15] = src[core, 15]

    every = slice(None)
    get_b.wait()
    b2 = split2(b_v[...]).T
    get_c.wait()
    p2 = split2(fold(nn(c_v[...], b2).T))
    get_a.wait()

    def first_pass(p, n=4):
        for k in range(n):
            get_e(n * p + k).wait()
        rows = pl.ds(pl.multiple_of(p * (128 * n), 128 * n), 128 * n)
        cols = jnp.concatenate([a_v[:, columns(n * p + k)] for k in range(n)], axis=1)
        part = fold(nn(e_v[rows, :], b2).T + nn(p2, cols))
        for h in range(2):
            for k in range(n):
                lt[h, n * p + k] = part[16 * h : 16 * h + 16, 128 * k : 128 * k + 128]

    @pl.loop(0, 2)
    def _(p):
        first_pass(p)

    pl.semaphore_wait(barrier, 38)

    @pl.loop(0, 8)
    def _(i):
        scatter(0, lt, rrec1, i)

    @pl.loop(4, 7)
    def _(p):
        first_pass(p, 2)
        for k in range(2):
            scatter(0, lt, rrec1, 2 * p + k)

    first_pass(7, 2)
    for i in range(14, 16):
        scatter(0, lt, rrec1, i)

    def finish(n, rrec, chunk, zrec, total, gat, gr, meanwhile):
        took(rrec.at[pl.ds(0, 31)], rr.at[n])
        acc = rrec[0]
        for i in range(1, 32):
            acc = acc + rrec[i]
        chunk[...] = acc
        for dz in ZOFF:
            remote(chunk, zrec.at[z], send.at[1 + 3 * n], zr.at[n], at(0, 0, dz, core)).start()
        zrec[z] = acc
        result = meanwhile()
        took(zrec.at[pl.ds(0, 7)], zr.at[n])
        acc = zrec[0]
        for k in range(1, 8):
            acc = acc + zrec[k]
        total[...] = acc
        for i in ORDER:
            dx, dy = OFF[i]
            slot = NEG[i]
            sem = gr.at[0 if slot in FAR else 1 if slot > 8 else 2]
            remote(total, gat.at[core, slot], send.at[2 + 3 * n], sem, at(dx, dy, 0, core)).start()
        for i in ORDER[:5]:
            dx, dy = OFF[i]
            remote(
                total, gat.at[core, NEG[i]], send.at[2 + 3 * n], gr.at[0], at(dx, dy, 0, other)
            ).start()
        remote(total, gat.at[core, 15], send.at[2 + 3 * n], gr.at[3], at(0, 0, 0, other)).start()
        gat[core, 15] = acc

        took(gat.at[core, pl.ds(9, 6)], gr.at[1])
        hand_on(gat, pl.ds(9, 6), 6 + n, gr.at[4])
        took(gat.at[core, pl.ds(3, 4)], gr.at[2])
        hand_on(gat, pl.ds(5, 3), 6 + n, gr.at[5])
        hand_on(gat, pl.ds(3, 1), 6 + n, gr.at[5])
        return result

    def hand_on(gat, blocks, s, r):
        part = gat.at[core, blocks]
        remote(part, part, send.at[s], r, at(0, 0, 0, other)).start()

    def gathered(first, last, gat):
        return jnp.concatenate(
            [jnp.concatenate([gat[0, i], gat[1, i]], axis=0) for i in range(first, last)], axis=1
        )

    def near_blocks(gat, gr):
        took(gat.at[other, pl.ds(9, 6)], gr.at[4])
        took(gat.at[other, 15], gr.at[3])

    def far_blocks(gat, gr):
        took(gat.at[0, pl.ds(0, 10)], gr.at[0])

    def last_blocks(gat, gr):
        took(gat.at[other, pl.ds(3, 4)], gr.at[5])

    @pl.loop(0, 8)
    def _(p):
        at_v[pl.ds(pl.multiple_of(p * 256, 256), 256), :] = both(a_v, every, p).T

    finish(0, rrec1, chunk1, zrec1, sum1, gat1, gr1, lambda: None)

    def accumulate(first, last, new):
        rows = slice(128 * first, 128 * last)
        l2 = split2(gathered(first, last, gat1))
        for j in range(4):
            cols = slice(512 * j, 512 * j + 512)
            part = nn(l2, e_v[rows, cols])
            zacc[:, cols] = part if new else zacc[:, cols] + part
        return nn(l2, at_v[rows, :])

    near_blocks(gat1, gr1)
    image = accumulate(10, 16, True)
    far_blocks(gat1, gr1)
    image = image + accumulate(8, 10, False) + accumulate(0, 2, False)
    last_blocks(gat1, gr1)
    rows = slice(256, 1024)
    l2 = split2(gathered(2, 8, gat1))
    image = image + nn(l2, at_v[rows, :])
    i2 = split2(fold(image))

    def second_pass(j):
        part = fold(both(zacc, every, j) + nn(l2, both(e_v, rows, j)) + nn(i2, both(c_v, every, j)))
        for h in range(2):
            for k in range(2):
                zt[h, 2 * j + k] = part[16 * h : 16 * h + 16, 128 * k : 128 * k + 128]
        scatter(1, zt, rrec2, 2 * j)
        scatter(1, zt, rrec2, 2 * j + 1)

    @pl.loop(0, 7)
    def _(j):
        second_pass(j)

    second_pass(7)

    for i in range(16):
        block = gathered(i, i + 1, gat1)
        left_abs[place(i)] = block
        stack[:, columns(i)] = jnp.concatenate(split3(block), axis=0)
    products = nt(stack[...], stack[...])

    def piece(r, c):
        return products[32 * r : 32 * r + 32, 32 * c : 32 * c + 32]

    gram = piece(0, 0) + (piece(0, 1) + piece(1, 0)) + (piece(1, 1) + piece(0, 2) + piece(2, 0))
    inverse = inverse_cholesky(gram)

    def factors():
        me = g * 64 + d
        basis_blk[...] = nn(left_stack(inverse), right_stack(left_abs[lax.div(me, 16)])).T
        own = left_stack(basis_blk[pl.ds(pl.multiple_of(lax.rem(me, 16) * 8, 8), 8), :])
        return left_stack(jnp.concatenate([inverse, nn(own, right_stack(inverse))], axis=0))

    both_factors = finish(1, rrec2, chunk2, zrec2, sum2, gat2, gr2, factors)
    near_blocks(gat2, gr2)
    far_blocks(gat2, gr2)
    last_blocks(gat2, gr2)
    for q in range(4):
        result = nn(both_factors, right_stack(gathered(4 * q, 4 * q + 4, gat2)))
        update = result[32:].astype(BF16)
        for k in range(4):
            lanes = slice(128 * k, 128 * k + 128)
            right_ref[:, columns(4 * q + k)] = result[:32, lanes]
            upd_ref[:, columns(4 * q + k)] = update[:, lanes]

    for n, rrec, zrec, gat in ((0, rrec1, zrec1, gat1), (1, rrec2, zrec2, gat2)):
        took(rrec.at[pl.ds(0, 31)], send.at[3 * n])
        took(zrec.at[pl.ds(0, 7)], send.at[1 + 3 * n])
        took(gat.at[0], send.at[2 + 3 * n])
        took(gat.at[0, pl.ds(0, 5)], send.at[2 + 3 * n])
        took(gat.at[0, pl.ds(0, 10)], send.at[6 + n])


def local(activations, cotangent, error_buffer, basis_start):
    vm = pltpu.VMEM
    dma = pltpu.SemaphoreType.DMA
    chunk = (16, 128)
    update, right = pl.pallas_call(
        kernel,
        out_shape=(jax.ShapeDtypeStruct((8, 2048), BF16), jax.ShapeDtypeStruct((32, 2048), F32)),
        in_specs=[pl.BlockSpec(memory_space=pltpu.HBM)] * 4,
        out_specs=[pl.BlockSpec(memory_space=pltpu.VMEM)] * 2,
        scratch_shapes=[
            vm((512, 2048), BF16), vm((512, 2048), BF16), vm((2048, 2048), BF16), vm((32, 2048), F32),
            vm((2048, 512), BF16), vm((2, 16) + chunk, F32), vm((2, 16) + chunk, F32),
            vm((32,) + chunk, F32), vm((32,) + chunk, F32), vm(chunk, F32), vm(chunk, F32),
            vm((8,) + chunk, F32), vm((8,) + chunk, F32), vm(chunk, F32), vm(chunk, F32),
            vm((2, 16) + chunk, F32), vm((2, 16) + chunk, F32),
            vm((64, 2048), F32), vm((96, 2048), BF16), vm((16, 32, 128), F32), vm((128, 32), F32),
            dma((19,)), dma((2,)), dma((2,)), dma((6,)), dma((6,)), dma((8,)),
        ],
        compiler_params=pltpu.CompilerParams(
            collective_id=0, has_side_effects=True, vmem_limit_bytes=56098816
        ),
        name="powersgd",
    )(activations, cotangent, error_buffer, basis_start.T)
    return update, right.T


def solution(mesh):
    placed = (P(("grp", "dp"), None), P(("grp", "dp"), None), P(("grp", "dp"), None), P())
    return jax.shard_map(
        local, mesh=mesh, in_specs=placed, out_specs=(P(("grp", "dp"), None), P()), check_vma=False
    )
```
